32 devices in a mesh: dp: 16 (over z, x, core), mp: 2 (over y).
Axes of the slice: x: 2, y: 2, z: 4, core: 2. Of those that a mesh axis runs over, the one named last changes fastest.
Arguments:
- tokens: bfloat16 [16384, 1024], P(('dp', 'mp')), may hold values from -6 to 6
- w_query: bfloat16 [1024, 1024], P('dp', 'mp'), may hold values from -0.1875 to 0.1875
- w_key: bfloat16 [1024, 1024], P('dp', 'mp'), may hold values from -0.1875 to 0.1875
- w_value: bfloat16 [1024, 1024], P('dp', 'mp'), may hold values from -0.1875 to 0.1875
- w_out: bfloat16 [1024, 1024], P('dp', 'mp'), may hold values from -1.5 to 1.5
- w_up: bfloat16 [1024, 4096], P('dp', 'mp'), may hold values from -0.1875 to 0.1875
- w_down: bfloat16 [1024, 4096], P('dp', 'mp'), may hold values from -0.09375 to 0.09375
- b_query: bfloat16 [1024], P('dp'), may hold values from -3 to 3
- b_value: bfloat16 [1024], P('dp'), may hold values from -3 to 3
- b_up: bfloat16 [4096], P('dp'), may hold values from -3 to 3
- b_out: bfloat16 [1024], P('dp'), may hold values from -2 to 2
- b_down: bfloat16 [1024], P('dp'), may hold values from -2 to 2
- gain_attn: bfloat16 [1024], P('dp'), may hold values from 0.25 to 1.75
- shift_attn: bfloat16 [1024], P('dp'), may hold values from -2 to 2
- gain_ffn: bfloat16 [1024], P('dp'), may hold values from 0.25 to 1.75
- shift_ffn: bfloat16 [1024], P('dp'), may hold values from -2 to 2
- out_grad: bfloat16 [16384, 1024], P(('dp', 'mp')), may hold values from -6 to 6
- seq_len: int32 [64], replicated, may hold values from 0 to 1024, as said below
- seq_group: int32 [64], replicated, may hold values from 0 to 15, as said below
- seq_start: int32 [64], replicated, may hold values from 0 to 1024, as said below
Outputs:
- layer_out: bfloat16 [16384, 1024], P(('dp', 'mp'))
- grad_tokens: float32 [16384, 1024], P(('dp', 'mp'))
- grad_w_query: float32 [1024, 1024], P('dp', 'mp')
- grad_w_key: float32 [1024, 1024], P('dp', 'mp')
- grad_w_value: float32 [1024, 1024], P('dp', 'mp')
- grad_w_out: float32 [1024, 1024], P('dp', 'mp')
- grad_w_up: float32 [1024, 4096], P('dp', 'mp')
- grad_w_down: float32 [1024, 4096], P('dp', 'mp')
- grad_b_query: float32 [1024], P('dp')
- grad_b_value: float32 [1024], P('dp')
- grad_b_up: float32 [4096], P('dp')
- grad_b_out: float32 [1024], P('dp')
- grad_b_down: float32 [1024], P('dp')
- grad_gain_attn: float32 [1024], P('dp')
- grad_shift_attn: float32 [1024], P('dp')
- grad_gain_ffn: float32 [1024], P('dp')
- grad_shift_ffn: float32 [1024], P('dp')
The draws below stay inside these ranges and needn't reach their ends.
Inputs may be any that keep to these rules, and one draw needn't show every extreme that they name: `seq_len`: each data group is named by exactly 4 slots; slots of length 0 are empty, the others hold 128 tokens or more; the slots of one group lie one after another from place 0 without intersection and within its 1024 places (an empty slot starts where the group's used places end); places not covered are padding; some group holds a single sequence of 1024 tokens. `seq_group`: which group holds which slot. `seq_start`: offsets as described for seq_len.
All inputs are finite; a program needn't handle non-finite values.
Results may differ from the reference program's by a relative error of at most 0.013.
The reference program's roundings to bfloat16 on the way count: a program that leaves them out, or rounds other values in their place, can miss the bound.
Values may be sent and summed in bfloat16 or wider, within the bound.
A program may use at most 192 MiB of HBM per device.

```python
import jax
import jax.numpy as jnp
from jax import lax

D = 1024
HEADS = 16
HDIM = 64
FF = 4096
MIN_LEN = 128
SLOTS = 4
GROUP = 1024
TOKENS = 16384
N_DP = 16


def deal_slots(key):
    count_key, length_key, full_key, order_key = jax.random.split(key, 4)
    groups = N_DP
    group_ids = jnp.arange(groups, dtype=jnp.int32)
    full_group = jax.random.randint(full_key, (), 0, groups)
    live_count = jax.random.randint(count_key, (groups,), 1, SLOTS + 1)
    live_count = jnp.where(group_ids == full_group, 1, live_count)
    upper = GROUP // live_count
    raw = jax.random.randint(length_key, (groups, SLOTS), 0, 1 << 30)
    lengths = MIN_LEN + raw % (upper[:, None] - MIN_LEN + 1)
    slot_place = jnp.arange(SLOTS, dtype=jnp.int32)[None, :]
    lengths = jnp.where(slot_place < live_count[:, None], lengths, 0)
    lengths = jnp.where((group_ids == full_group)[:, None] & (slot_place == 0), GROUP, lengths)
    lengths = lengths.astype(jnp.int32)
    starts = (jnp.cumsum(lengths, axis=1) - lengths).astype(jnp.int32)
    owners = jnp.broadcast_to(group_ids[:, None], (groups, SLOTS)).astype(jnp.int32)
    order = jax.random.permutation(order_key, groups * SLOTS)
    return (lengths.reshape(-1)[order], owners.reshape(-1)[order], starts.reshape(-1)[order])


def draw_seq_len(key, part):
    shared = deal_slots(key)
    return shared[0]


def draw_seq_group(key, part):
    shared = deal_slots(key)
    return shared[1]


def draw_seq_start(key, part):
    shared = deal_slots(key)
    return shared[2]


def spiked(values, own_key, source, target, shards_of, factor):
    def block_of(axis_at):
        return (jnp.arange(values.shape[axis_at]) // (values.shape[axis_at] // shards_of)).reshape((-1,) + (1,) * (values.ndim - 1 - axis_at))

    near = jax.random.permutation(own_key, shards_of)[block_of(target)]
    other_side = (block_of(target) + shards_of // 2) % shards_of
    return jnp.where((block_of(source) == near) | (block_of(source) == other_side), factor * values, values)


def level_of(stream_key, extent, pieces, smallest, high):
    loudness, own = 1.0, jax.random.fold_in(stream_key, 6)
    for axis_at, blocks in pieces:
        steps = jnp.exp(jax.random.uniform(jax.random.fold_in(own, axis_at), (blocks,), jnp.float32, smallest / len(pieces), high / len(pieces)))
        loudness = loudness * jnp.repeat(steps, extent[axis_at] // blocks).reshape([-1 if axis == axis_at else 1 for axis in range(len(extent))])
    return loudness


def scatter_about(key, dims, width, most, cuts=(), held_as=jnp.bfloat16):
    values = jax.random.normal(key, dims, jnp.float32) * width
    if len(cuts) > 0:
        values = level_of(key, dims, cuts, -0.22, 0.18) * values
    return jnp.clip(values, min=-most, max=most).astype(held_as)


def noise_with(stream_key, shape, width, limit, cuts, heavy, kind=jnp.bfloat16):
    entries = width * jax.random.normal(stream_key, shape, jnp.float32)
    if cuts:
        entries = entries * level_of(stream_key, shape, cuts, -0.22, 0.18)
    return jnp.clip(spiked(entries, jax.random.fold_in(stream_key, 3), *heavy), -limit, limit).astype(kind)


def setup_inputs(seed: int = 0) -> dict:
    streams_of = jax.random.split(jax.random.key(seed), 21)
    tokens = noise_with(streams_of[0], (TOKENS, D), 1.0, 6.0, ((0, 32),), (0, 1, 32, 2.75))
    w_query = scatter_about(streams_of[1], (D, D), D ** -0.5, 0.1875, ((0, 16), (1, 2)))
    w_key = scatter_about(streams_of[2], (D, D), D ** -0.5, 0.1875, ((0, 16), (1, 2)))
    w_value = scatter_about(streams_of[3], (D, D), D ** -0.5, 0.1875, ((0, 16), (1, 2)))
    w_out = scatter_about(streams_of[4], (D, D), (D // 64) ** -0.5, 1.5, ((0, 16), (1, 2)))
    w_up = scatter_about(streams_of[5], (D, FF), D ** -0.5, 0.1875, ((0, 16), (1, 2)))
    w_down = scatter_about(streams_of[6], (D, FF), FF ** -0.5, 0.09375, ((0, 16), (1, 2)))
    b_query = scatter_about(streams_of[7], (D,), 0.5, 3.0, ((0, 16),))
    b_value = scatter_about(streams_of[8], (D,), 0.5, 3.0, ((0, 16),))
    b_up = scatter_about(streams_of[9], (FF,), 0.5, 3.0, ((0, 16),))
    b_out = scatter_about(streams_of[10], (D,), 0.3, 2.0, ((0, 16),))
    b_down = scatter_about(streams_of[11], (D,), 0.3, 2.0, ((0, 16),))
    gain_attn = jnp.clip(1.0 + 0.15 * jax.random.normal(streams_of[12], (D,), jnp.float32), 0.25, 1.75).astype(jnp.bfloat16)
    shift_attn = scatter_about(streams_of[13], (D,), 0.3, 2.0, ((0, 16),))
    gain_ffn = jnp.clip(1.0 + 0.15 * jax.random.normal(streams_of[14], (D,), jnp.float32), 0.25, 1.75).astype(jnp.bfloat16)
    shift_ffn = scatter_about(streams_of[15], (D,), 0.3, 2.0, ((0, 16),))
    out_grad = scatter_about(streams_of[16], (TOKENS, D), 1.0, 6.0, ((0, 32),))
    seq_len = draw_seq_len(jax.random.fold_in(streams_of[20], 71), 0)
    seq_group = draw_seq_group(jax.random.fold_in(streams_of[20], 71), 0)
    seq_start = draw_seq_start(jax.random.fold_in(streams_of[20], 71), 0)
    return dict(tokens=tokens, w_query=w_query, w_key=w_key, w_value=w_value, w_out=w_out, w_up=w_up, w_down=w_down, b_query=b_query, b_value=b_value, b_up=b_up, b_out=b_out, b_down=b_down, gain_attn=gain_attn, shift_attn=shift_attn, gain_ffn=gain_ffn, shift_ffn=shift_ffn, out_grad=out_grad, seq_len=seq_len, seq_group=seq_group, seq_start=seq_start)


@jax.custom_vjp
def low(v):
    return lax.optimization_barrier(v.astype(jnp.bfloat16)).astype(jnp.float32)

@jax.custom_vjp
def low_back(v):
    return v

def low_keep(v):
    return (low(v), None)

def low_pass(kept, grad):
    return (grad,)

def back_keep(v):
    return (v, None)

def back_low(kept, grad):
    return (low(grad),)
low.defvjp(low_keep, low_pass)
low_back.defvjp(back_keep, back_low)
eps = 1e-05
masked_score = -1e+30
highest = lax.Precision.HIGHEST

def rounded_both(values):
    return low_back(low(values))

def norm_rows(values, gain, shift):
    center = values - lax.optimization_barrier(jnp.mean(values, axis=-1, keepdims=True))
    spread = lax.optimization_barrier(jnp.mean(center * center, axis=-1, keepdims=True))
    return center * lax.rsqrt(spread + eps) * gain + shift

def token_segments(group_id, group_rows, seq_len, seq_group, seq_start):
    places = jnp.arange(group_rows, dtype=jnp.int32)[None, :]
    starts = seq_start[:, None]
    inside = (seq_group[:, None] == group_id) & (places >= starts) & (places < starts + seq_len[:, None])
    labels = jnp.arange(1, seq_len.shape[0] + 1, dtype=jnp.int32)[:, None]
    return lax.optimization_barrier(jnp.sum(jnp.where(inside, labels, 0), axis=0)).astype(jnp.int32) - 1

def group_layer(params, rows, segment):
    w_query, w_key, w_value, w_out, w_up, w_down, b_query, b_value, b_up, b_out, b_down, gain_attn, shift_attn, gain_ffn, shift_ffn = params
    count = rows.shape[0]
    query = rounded_both(jnp.dot(rows, w_query, precision=highest) + b_query).reshape(count, HEADS, HDIM)
    keys = rounded_both(jnp.dot(rows, w_key, precision=highest)).reshape(count, HEADS, HDIM)
    values = rounded_both(jnp.dot(rows, w_value, precision=highest) + b_value).reshape(count, HEADS, HDIM)
    scores = low_back(jnp.einsum('qhd,khd->hqk', query, keys, precision=highest) * HDIM ** (-0.5))
    same_doc = segment[:, None] == segment[None, :]
    scores = jnp.where(same_doc[None], scores, masked_score)
    row_max = lax.optimization_barrier(jnp.max(scores, axis=-1, keepdims=True))
    shifted = jnp.exp(scores - row_max)
    probs = shifted / lax.optimization_barrier(jnp.sum(shifted, axis=-1, keepdims=True))
    context = jnp.einsum('hqk,khd->qhd', low(probs), values, precision=highest).reshape(count, D)
    context = rounded_both(context)
    attended = low_back(jnp.dot(context, w_out.T, precision=highest))
    first = norm_rows(rows + attended + b_out, gain_attn, shift_attn)
    hidden = low_back(jnp.dot(low(first), w_up, precision=highest) + b_up)
    active = low(jax.nn.gelu(hidden, approximate=False))
    branch = low_back(jnp.dot(active, w_down.T, precision=highest))
    return norm_rows(first + branch + b_down, gain_ffn, shift_ffn)

def reference(tokens, w_query, w_key, w_value, w_out, w_up, w_down, b_query, b_value, b_up, b_out, b_down, gain_attn, shift_attn, gain_ffn, shift_ffn, out_grad, seq_len, seq_group, seq_start):
    params = tuple((item.astype(jnp.float32) for item in (w_query, w_key, w_value, w_out, w_up, w_down, b_query, b_value, b_up, b_out, b_down, gain_attn, shift_attn, gain_ffn, shift_ffn)))
    blocks = tokens.astype(jnp.float32).reshape(N_DP, GROUP, D)
    cotangents = out_grad.astype(jnp.float32).reshape(N_DP, GROUP, D)

    def one_group(totals, inputs):
        group_id, rows, cotan = inputs
        segment = token_segments(group_id, GROUP, seq_len, seq_group, seq_start)
        alive = (segment >= 0).astype(jnp.float32)[:, None]
        result, pullback = jax.vjp(lambda prm, xrows: group_layer(prm, xrows, segment), params, rows)
        grad_params, grad_rows = pullback(cotan * alive)
        totals = jax.tree.map(lambda left, right: left + right, totals, grad_params)
        return (totals, (result * alive, grad_rows))
    zeros = jax.tree.map(jnp.zeros_like, params)
    totals, (results, grad_rows) = lax.scan(one_group, zeros, (jnp.arange(N_DP, dtype=jnp.int32), blocks, cotangents))
    layer_out = results.reshape(TOKENS, D).astype(jnp.bfloat16)
    grad_tokens = grad_rows.reshape(TOKENS, D)
    return (layer_out, grad_tokens, totals[0], totals[1], totals[2], totals[3], totals[4], totals[5], totals[6], totals[7], totals[8], totals[9], totals[10], totals[11], totals[12], totals[13], totals[14])
```

```python
import jax
import jax.numpy as jnp
from jax import lax
from jax.experimental import pallas as pl
from jax.experimental.pallas import tpu as pltpu
from jax.sharding import Mesh, PartitionSpec as P

HDIM = 64
PAIR = 2 * HDIM
eps = 1e-05
masked_score = -1e30
scale = HDIM ** (-0.5)
f32 = jnp.float32
bf16 = jnp.bfloat16
NT = (((1,), (1,)), ((), ()))
NN = (((1,), (0,)), ((), ()))
TN = (((0,), (0,)), ((), ()))


def mm(left, right, dims=NN):
    return lax.dot_general(left, right, dims, preferred_element_type=f32)


def head_lanes(rows, head):
    lane = lax.broadcasted_iota(jnp.int32, (rows, PAIR), 1)
    return (lane >= head * HDIM) & (lane < (head + 1) * HDIM)


def attn_fwd_kernel(seg_col, seg_row, q_ref, k_ref, v_ref, ctx_ref, lse_ref):
    rows = q_ref.shape[0]
    same = seg_col[...] == seg_row[...]
    q = q_ref[...] * jnp.asarray(scale, bf16)
    k = k_ref[...]
    v = v_ref[...]
    first = head_lanes(rows, 0)
    parts = []
    for head in range(2):
        qh = jnp.where(head_lanes(rows, head), q, jnp.zeros_like(q))
        scores = jnp.where(same, mm(qh, k, NT), masked_score)
        top = jnp.max(scores, axis=-1, keepdims=True)
        shifted = jnp.exp(scores - top)
        total = jnp.sum(shifted, axis=-1, keepdims=True)
        piece = mm(shifted.astype(bf16), v) * (1.0 / total)
        parts.append((piece, top + jnp.log(total)))
    ctx_ref[...] = jnp.where(first, parts[0][0], parts[1][0]).astype(bf16)
    lse_ref[...] = jnp.where(first, parts[0][1], parts[1][1])


def attn_bwd_kernel(
    seg_col, seg_row, lse_ref, q_ref, k_ref, v_ref, do_ref, dq_ref, dk_ref, dv_ref, dk_acc, dv_acc
):
    block = pl.program_id(1)

    @pl.when(block == 0)
    def _():
        dk_acc[...] = jnp.zeros_like(dk_acc)
        dv_acc[...] = jnp.zeros_like(dv_acc)

    rows = q_ref.shape[0]
    same = seg_col[...] == seg_row[...]
    q = q_ref[...] * jnp.asarray(scale, bf16)
    k = k_ref[...]
    v = v_ref[...]
    do = do_ref[...]
    parts = []
    for head in range(2):
        lanes = head_lanes(rows, head)
        qh = jnp.where(lanes, q, jnp.zeros_like(q))
        doh = jnp.where(lanes, do, jnp.zeros_like(do))
        lse = lse_ref[:, head * HDIM : head * HDIM + 1]
        scores = jnp.where(same, mm(qh, k, NT), masked_score)
        probs = jnp.exp(scores - lse)
        d_probs = mm(doh, v, NT)
        delta = jnp.sum(probs * d_probs, axis=-1, keepdims=True)
        d_scores = (probs * (d_probs - delta)).astype(bf16)
        parts.append(mm(d_scores, k) * scale)
        dk_acc[...] += mm(qh, d_scores, TN)
        dv_acc[...] += mm(doh, probs.astype(bf16), TN)
    dq_ref[...] = jnp.where(head_lanes(rows, 0), parts[0], parts[1]).astype(bf16)

    @pl.when(block == pl.num_programs(1) - 1)
    def _():
        dk_ref[...] = dk_acc[...].T.astype(bf16)
        dv_ref[...] = dv_acc[...].T.astype(bf16)


def attn_specs(rows, pairs, block):
    return (
        pl.BlockSpec((block, 1), lambda h, j: (j, 0)),
        pl.BlockSpec((1, rows), lambda h, j: (0, 0)),
        pl.BlockSpec((block, PAIR), lambda h, j: (j, h)),
        pl.BlockSpec((rows, PAIR), lambda h, j: (0, pairs + h)),
        pl.BlockSpec((rows, PAIR), lambda h, j: (0, 2 * pairs + h)),
    )


def attn_params():
    return pltpu.CompilerParams(
        dimension_semantics=("arbitrary", "arbitrary"), vmem_limit_bytes=56 * 1024 * 1024
    )


def attn_fwd(qkv, seg):
    rows = qkv.shape[0]
    width = qkv.shape[1] // 3
    pairs = width // PAIR
    block = min(512, rows)
    col, row, qs, ks, vs = attn_specs(rows, pairs, block)
    per_block = pl.BlockSpec((block, PAIR), lambda h, j: (j, h))
    return pl.pallas_call(
        attn_fwd_kernel,
        grid=(pairs, rows // block),
        in_specs=[col, row, qs, ks, vs],
        out_specs=[per_block, per_block],
        out_shape=[
            jax.ShapeDtypeStruct((rows, width), bf16),
            jax.ShapeDtypeStruct((rows, width), f32),
        ],
        compiler_params=attn_params(),
        cost_estimate=pl.CostEstimate(
            flops=8 * rows * rows * width,
            bytes_accessed=rows * width * 12,
            transcendentals=rows * rows * width // HDIM,
        ),
        name="attn_fwd",
    )(seg[:, None], seg[None, :], qkv, qkv, qkv)


def attn_bwd(qkv, seg, lse, do):
    rows = qkv.shape[0]
    width = qkv.shape[1] // 3
    pairs = width // PAIR
    block = min(512, rows)
    col, row, qs, ks, vs = attn_specs(rows, pairs, block)
    per_block = pl.BlockSpec((block, PAIR), lambda h, j: (j, h))
    whole = pl.BlockSpec((rows, PAIR), lambda h, j: (0, h))
    return pl.pallas_call(
        attn_bwd_kernel,
        grid=(pairs, rows // block),
        in_specs=[col, row, per_block, qs, ks, vs, per_block],
        out_specs=[per_block, whole, whole],
        out_shape=[jax.ShapeDtypeStruct((rows, width), bf16)] * 3,
        scratch_shapes=[pltpu.VMEM((PAIR, rows), f32), pltpu.VMEM((PAIR, rows), f32)],
        compiler_params=attn_params(),
        cost_estimate=pl.CostEstimate(
            flops=20 * rows * rows * width,
            bytes_accessed=rows * width * 18,
            transcendentals=rows * rows * width // HDIM,
        ),
        name="attn_bwd",
    )(seg[:, None], seg[None, :], lse, qkv, qkv, qkv, do)


def norm_parts(values):
    center = values - jnp.mean(values, axis=-1, keepdims=True)
    factor = lax.rsqrt(jnp.mean(center * center, axis=-1, keepdims=True) + eps)
    return center * factor, factor


def norm_back(cot, normed, factor, gain):
    e = cot * gain
    mean_e = jnp.mean(e, axis=-1, keepdims=True)
    mean_en = jnp.mean(e * normed, axis=-1, keepdims=True)
    return factor * (e - mean_e - normed * mean_en)


def token_segments(group_id, places, seq_len, seq_group, seq_start):
    places = places[None, :]
    starts = seq_start[:, None]
    inside = (
        (seq_group[:, None] == group_id) & (places >= starts) & (places < starts + seq_len[:, None])
    )
    labels = jnp.arange(1, seq_len.shape[0] + 1, dtype=jnp.int32)[:, None]
    return jnp.sum(jnp.where(inside, labels, 0), axis=0) - 1


def gelu_parts(hidden):
    cdf = 0.5 * (1.0 + lax.erf(hidden * (0.5**0.5)))
    slope = cdf + hidden * jnp.exp(-0.5 * hidden * hidden) * (0.5 / jnp.pi) ** 0.5
    return hidden * cdf, slope


def turned(x):
    return lax.ppermute(x, ("core", "y"), [(0, 0), (1, 2), (2, 1), (3, 3)])


def partner(x):
    return lax.ppermute(x, "core", [(0, 1), (1, 0)])


def local(
    tokens,
    w_query,
    w_key,
    w_value,
    w_out,
    w_up,
    w_down,
    b_query,
    b_value,
    b_up,
    b_out,
    b_down,
    gain_attn,
    shift_attn,
    gain_ffn,
    shift_ffn,
    out_grad,
    seq_len,
    seq_group,
    seq_start,
):
    half = tokens.shape[0]
    core = lax.axis_index("core")
    group = lax.axis_index("pair") * 2 + lax.axis_index("y")
    owner = lax.axis_index("pair") * 2 + core
    width = w_query.shape[1]
    hidden_width = w_up.shape[1]

    def gather(x):
        return lax.all_gather(x, ("pair", "y"), axis=0, tiled=True)

    def scatter(x):
        part = lax.psum_scatter(x.astype(bf16), ("pair", "y"), scatter_dimension=0, tiled=True)
        return turned(part).astype(f32)

    qkv_mat = gather(turned(jnp.concatenate([w_query, w_key, w_value], axis=1)))
    small = (b_query, b_value, b_out, b_down, gain_attn, shift_attn, gain_ffn, shift_ffn, b_up)
    vectors = lax.all_gather(jnp.concatenate(small), ("pair", "core"), axis=0, tiled=False)
    own = turned(tokens)
    rows_all = jnp.concatenate([own, partner(own)], axis=0)
    out_mat = gather(turned(w_out))
    up_mat = gather(turned(w_up))
    down_mat = gather(turned(w_down))
    cot_rows = turned(out_grad)

    piece = b_query.shape[0]
    full = [
        vectors[:, i * piece : (i + 1) * piece].reshape(-1).astype(f32) for i in range(8)
    ]
    up_bias = vectors[:, 8 * piece :].reshape(-1).astype(f32)
    query_bias, value_bias, out_bias, down_bias, gain_one, shift_one, gain_two, shift_two = full
    query_local = lax.dynamic_slice_in_dim(query_bias, core * width, width)
    value_local = lax.dynamic_slice_in_dim(value_bias, core * width, width)
    up_local = lax.dynamic_slice_in_dim(up_bias, core * hidden_width, hidden_width)
    qkv_bias = jnp.concatenate([query_local, jnp.zeros((width,), f32), value_local])

    places = jnp.arange(half, dtype=jnp.int32)
    places = jnp.concatenate([places + core * half, places + (1 - core) * half])
    seg = token_segments(group, places, seq_len, seq_group, seq_start)
    alive = (seg[:half] >= 0).astype(f32)[:, None]

    qkv = (mm(rows_all, qkv_mat) + qkv_bias).astype(bf16)
    context, lse = attn_fwd(qkv, seg)

    def summed_rows(left, right, dims):
        sent = partner(mm(left[half:], right, dims).astype(bf16))
        return mm(left[:half], right, dims) + sent.astype(f32)

    attended = summed_rows(context, out_mat, NT)
    n1, r1 = norm_parts(own.astype(f32) + attended + out_bias)
    first = n1 * gain_one + shift_one
    first_own = first.astype(bf16)
    first_all = jnp.concatenate([first_own, partner(first_own)], axis=0)
    hidden = mm(first_all, up_mat) + up_local
    active = gelu_parts(hidden)[0].astype(bf16)
    branch = summed_rows(active, down_mat, NT)
    n2, r2 = norm_parts(first + branch + down_bias)
    layer_out = turned(((n2 * gain_two + shift_two) * alive).astype(bf16))

    cot = cot_rows.astype(f32) * alive
    d_second = norm_back(cot, n2, r2, gain_two)
    d_branch_own = d_second.astype(bf16)
    d_branch = jnp.concatenate([d_branch_own, partner(d_branch_own)], axis=0)
    d_hidden = (mm(d_branch, down_mat) * gelu_parts(hidden)[1]).astype(bf16)
    grad_down = scatter(mm(d_branch, active, TN))
    d_first = d_second + summed_rows(d_hidden, up_mat, NT)
    grad_up = scatter(mm(first_all, d_hidden, TN))
    d_first_in = norm_back(d_first, n1, r1, gain_one)
    d_attn_own = d_first_in.astype(bf16)
    d_attn = jnp.concatenate([d_attn_own, partner(d_attn_own)], axis=0)
    d_context = mm(d_attn, out_mat).astype(bf16)
    grad_out = scatter(mm(d_attn, context, TN))
    d_query, d_keys, d_values = attn_bwd(qkv, seg, lse, d_context)
    d_qkv = jnp.concatenate([d_query, d_keys, d_values], axis=1)
    grad_qkv = scatter(mm(rows_all, d_qkv, TN))
    d_rows = d_first_in + summed_rows(d_qkv, qkv_mat, NT)
    grad_tokens = turned(d_rows.astype(bf16)).astype(f32)

    def widen(vector):
        total = jnp.zeros((2 * vector.shape[0],), f32)
        return lax.dynamic_update_slice_in_dim(total, vector, core * vector.shape[0], 0)

    sums = (
        widen(jnp.sum(d_query.astype(f32), axis=0)),
        widen(jnp.sum(d_values.astype(f32), axis=0)),
        jnp.sum(d_first_in, axis=0),
        jnp.sum(d_second, axis=0),
        jnp.sum(d_first * n1, axis=0),
        jnp.sum(d_first, axis=0),
        jnp.sum(cot * n2, axis=0),
        jnp.sum(cot, axis=0),
        widen(jnp.sum(d_hidden.astype(f32), axis=0)),
    )
    packed = jnp.concatenate([item.reshape(vectors.shape[0], -1) for item in sums], axis=1)
    totals = lax.psum(packed, ("pair", "core", "y"))
    mine = lax.dynamic_index_in_dim(totals, owner, 0, keepdims=False)
    parts = [mine[i * piece : (i + 1) * piece] for i in range(8)]
    grad_b_query, grad_b_value, grad_b_out, grad_b_down = parts[:4]
    return (
        layer_out,
        grad_tokens,
        grad_qkv[:, :width],
        grad_qkv[:, width : 2 * width],
        grad_qkv[:, 2 * width :],
        grad_out,
        grad_up,
        grad_down,
        grad_b_query,
        grad_b_value,
        mine[8 * piece :],
        grad_b_out,
        grad_b_down,
        parts[4],
        parts[5],
        parts[6],
        parts[7],
    )


def solution(mesh):
    dp, mp = mesh.devices.shape
    folded = Mesh(mesh.devices.reshape(dp // 2, 2, mp), ("pair", "core", "y"))
    rows = P(("pair", "core", "y"), None)
    weight = P(("pair", "core"), "y")
    vector = P(("pair", "core"))
    placed = (rows,) + (weight,) * 6 + (vector,) * 9 + (rows,) + (P(),) * 3
    return jax.shard_map(
        local,
        mesh=folded,
        in_specs=placed,
        out_specs=(rows, rows) + (weight,) * 6 + (vector,) * 9,
        check_vma=False,
    )
```

```python
import jax
import jax.numpy as jnp
from jax import lax
from jax.experimental import pallas as pl
from jax.experimental.pallas import tpu as pltpu
from jax.sharding import Mesh, PartitionSpec as P

HDIM = 64
PAIR = 2 * HDIM
eps = 1e-05
masked_score = -1e30
scale = HDIM ** (-0.5)
f32 = jnp.float32
bf16 = jnp.bfloat16
NT = (((1,), (1,)), ((), ()))
NN = (((1,), (0,)), ((), ()))
TN = (((0,), (0,)), ((), ()))


def mm(left, right, dims=NN):
    return lax.dot_general(left, right, dims, preferred_element_type=f32)


def head_lanes(rows, head):
    lane = lax.broadcasted_iota(jnp.int32, (rows, PAIR), 1)
    return (lane >= head * HDIM) & (lane < (head + 1) * HDIM)


def attn_fwd_kernel(seg_col, seg_row, q_ref, k_ref, v_ref, ctx_ref, lse_ref):
    rows = q_ref.shape[0]
    same = seg_col[...] == seg_row[...]
    q = q_ref[...] * jnp.asarray(scale, bf16)
    k = k_ref[...]
    v = v_ref[...]
    first = head_lanes(rows, 0)
    parts = []
    for head in range(2):
        qh = jnp.where(head_lanes(rows, head), q, jnp.zeros_like(q))
        scores = jnp.where(same, mm(qh, k, NT), masked_score)
        top = jnp.max(scores, axis=-1, keepdims=True)
        shifted = jnp.exp(scores - top)
        total = jnp.sum(shifted, axis=-1, keepdims=True)
        piece = mm(shifted.astype(bf16), v) * (1.0 / total)
        parts.append((piece, top + jnp.log(total)))
    ctx_ref[...] = jnp.where(first, parts[0][0], parts[1][0]).astype(bf16)
    lse_ref[...] = jnp.where(first, parts[0][1], parts[1][1])


def attn_bwd_kernel(
    seg_col, seg_row, lse_ref, q_ref, k_ref, v_ref, do_ref, dq_ref, dk_ref, dv_ref, dk_acc, dv_acc
):
    block = pl.program_id(1)

    @pl.when(block == 0)
    def _():
        dk_acc[...] = jnp.zeros_like(dk_acc)
        dv_acc[...] = jnp.zeros_like(dv_acc)

    rows = q_ref.shape[0]
    same = seg_col[...] == seg_row[...]
    q = q_ref[...] * jnp.asarray(scale, bf16)
    k = k_ref[...]
    v = v_ref[...]
    do = do_ref[...]
    parts = []
    for head in range(2):
        lanes = head_lanes(rows, head)
        qh = jnp.where(lanes, q, jnp.zeros_like(q))
        doh = jnp.where(lanes, do, jnp.zeros_like(do))
        lse = lse_ref[:, head * HDIM : head * HDIM + 1]
        scores = jnp.where(same, mm(qh, k, NT), masked_score)
        probs = jnp.exp(scores - lse)
        d_probs = mm(doh, v, NT)
        delta = jnp.sum(probs * d_probs, axis=-1, keepdims=True)
        d_scores = (probs * (d_probs - delta)).astype(bf16)
        parts.append(mm(d_scores, k) * scale)
        dk_acc[...] += mm(qh, d_scores, TN)
        dv_acc[...] += mm(doh, probs.astype(bf16), TN)
    dq_ref[...] = jnp.where(head_lanes(rows, 0), parts[0], parts[1]).astype(bf16)

    @pl.when(block == pl.num_programs(1) - 1)
    def _():
        dk_ref[...] = dk_acc[...].T.astype(bf16)
        dv_ref[...] = dv_acc[...].T.astype(bf16)


def attn_specs(rows, pairs, block):
    return (
        pl.BlockSpec((block, 1), lambda h, j: (j, 0)),
        pl.BlockSpec((1, rows), lambda h, j: (0, 0)),
        pl.BlockSpec((block, PAIR), lambda h, j: (j, h)),
        pl.BlockSpec((rows, PAIR), lambda h, j: (0, pairs + h)),
        pl.BlockSpec((rows, PAIR), lambda h, j: (0, 2 * pairs + h)),
    )


def attn_params():
    return pltpu.CompilerParams(
        dimension_semantics=("arbitrary", "arbitrary"), vmem_limit_bytes=56 * 1024 * 1024
    )


def attn_fwd(qkv, seg):
    rows = qkv.shape[0]
    width = qkv.shape[1] // 3
    pairs = width // PAIR
    block = min(512, rows)
    col, row, qs, ks, vs = attn_specs(rows, pairs, block)
    per_block = pl.BlockSpec((block, PAIR), lambda h, j: (j, h))
    return pl.pallas_call(
        attn_fwd_kernel,
        grid=(pairs, rows // block),
        in_specs=[col, row, qs, ks, vs],
        out_specs=[per_block, per_block],
        out_shape=[
            jax.ShapeDtypeStruct((rows, width), bf16),
            jax.ShapeDtypeStruct((rows, width), f32),
        ],
        compiler_params=attn_params(),
        cost_estimate=pl.CostEstimate(
            flops=8 * rows * rows * width,
            bytes_accessed=rows * width * 12,
            transcendentals=rows * rows * width // HDIM,
        ),
        name="attn_fwd",
    )(seg[:, None], seg[None, :], qkv, qkv, qkv)


def attn_bwd(qkv, seg, lse, do):
    rows = qkv.shape[0]
    width = qkv.shape[1] // 3
    pairs = width // PAIR
    block = min(512, rows)
    col, row, qs, ks, vs = attn_specs(rows, pairs, block)
    per_block = pl.BlockSpec((block, PAIR), lambda h, j: (j, h))
    whole = pl.BlockSpec((rows, PAIR), lambda h, j: (0, h))
    return pl.pallas_call(
        attn_bwd_kernel,
        grid=(pairs, rows // block),
        in_specs=[col, row, per_block, qs, ks, vs, per_block],
        out_specs=[per_block, whole, whole],
        out_shape=[jax.ShapeDtypeStruct((rows, width), bf16)] * 3,
        scratch_shapes=[pltpu.VMEM((PAIR, rows), f32), pltpu.VMEM((PAIR, rows), f32)],
        compiler_params=attn_params(),
        cost_estimate=pl.CostEstimate(
            flops=20 * rows * rows * width,
            bytes_accessed=rows * width * 18,
            transcendentals=rows * rows * width // HDIM,
        ),
        name="attn_bwd",
    )(seg[:, None], seg[None, :], lse, qkv, qkv, qkv, do)


def norm_parts(values):
    center = values - jnp.mean(values, axis=-1, keepdims=True)
    factor = lax.rsqrt(jnp.mean(center * center, axis=-1, keepdims=True) + eps)
    return center * factor, factor


def norm_back(cot, normed, factor, gain):
    e = cot * gain
    mean_e = jnp.mean(e, axis=-1, keepdims=True)
    mean_en = jnp.mean(e * normed, axis=-1, keepdims=True)
    return factor * (e - mean_e - normed * mean_en)


def token_segments(group_id, places, seq_len, seq_group, seq_start):
    places = places[None, :]
    starts = seq_start[:, None]
    inside = (
        (seq_group[:, None] == group_id) & (places >= starts) & (places < starts + seq_len[:, None])
    )
    labels = jnp.arange(1, seq_len.shape[0] + 1, dtype=jnp.int32)[:, None]
    return jnp.sum(jnp.where(inside, labels, 0), axis=0) - 1


def gelu_parts(hidden):
    cdf = 0.5 * (1.0 + lax.erf(hidden * (0.5**0.5)))
    slope = cdf + hidden * jnp.exp(-0.5 * hidden * hidden) * (0.5 / jnp.pi) ** 0.5
    return hidden * cdf, slope


def turned(x):
    return lax.ppermute(x, ("core", "y"), [(0, 0), (1, 2), (2, 1), (3, 3)])


def partner(x):
    return lax.ppermute(x, "core", [(0, 1), (1, 0)])


def local(
    tokens,
    w_query,
    w_key,
    w_value,
    w_out,
    w_up,
    w_down,
    b_query,
    b_value,
    b_up,
    b_out,
    b_down,
    gain_attn,
    shift_attn,
    gain_ffn,
    shift_ffn,
    out_grad,
    seq_len,
    seq_group,
    seq_start,
):
    half = tokens.shape[0]
    core = lax.axis_index("core")
    group = lax.axis_index("pair") * 2 + lax.axis_index("y")
    width = w_query.shape[1]
    hidden_width = w_up.shape[1]

    side = lax.axis_index("y")
    pairs = lax.axis_size("pair")
    sheet = 16

    def across(x):
        return lax.ppermute(x, "y", [(0, 1), (1, 0)])

    def gather(x):
        shard = turned(x)
        mine = lax.all_gather(shard, "pair", axis=0, tiled=False)
        other = across(mine)
        low = jnp.where(side == 0, mine, other)
        high = jnp.where(side == 0, other, mine)
        return jnp.stack([low, high], axis=1)

    def scatter(x):
        blocks = x.reshape(pairs, 2, -1, x.shape[-1])
        sent = across(lax.dynamic_index_in_dim(blocks, 1 - side, 1, keepdims=False))
        kept = lax.dynamic_index_in_dim(blocks, side, 1, keepdims=False)
        total = (kept.astype(f32) + sent.astype(f32)).astype(bf16)
        total = total.reshape(-1, x.shape[-1])
        part = lax.psum_scatter(total, "pair", scatter_dimension=0, tiled=True)
        return turned(part).astype(f32)

    def whole_matrix(x):
        return x.reshape(-1, x.shape[-1])

    shard_rows = w_query.shape[0]
    small = (b_query, b_value, b_out, b_down, gain_attn, shift_attn, gain_ffn, shift_ffn, b_up)
    small = jnp.concatenate(small)
    small_size = small.shape[0]
    extra = jnp.pad(small[None, :], ((0, sheet - 1), (0, 3 * width - small_size)))
    qkv_shard = jnp.concatenate([w_query, w_key, w_value], axis=1)
    qkv_full = gather(jnp.concatenate([qkv_shard, extra], axis=0))
    qkv_mat = whole_matrix(qkv_full[:, :, :shard_rows])
    vectors = qkv_full[:, :, shard_rows, :small_size].reshape(-1, small_size)
    own = turned(tokens)
    rows_all = jnp.concatenate([own, partner(own)], axis=0)
    out_mat = whole_matrix(gather(w_out))
    up_mat = whole_matrix(gather(w_up))
    down_mat = whole_matrix(gather(w_down))
    cot_rows = turned(out_grad)

    piece = b_query.shape[0]
    full = [
        vectors[:, i * piece : (i + 1) * piece].reshape(-1).astype(f32) for i in range(8)
    ]
    up_bias = vectors[:, 8 * piece :].reshape(-1).astype(f32)
    query_bias, value_bias, out_bias, down_bias, gain_one, shift_one, gain_two, shift_two = full
    query_local = lax.dynamic_slice_in_dim(query_bias, core * width, width)
    value_local = lax.dynamic_slice_in_dim(value_bias, core * width, width)
    up_local = lax.dynamic_slice_in_dim(up_bias, core * hidden_width, hidden_width)
    qkv_bias = jnp.concatenate([query_local, jnp.zeros((width,), f32), value_local])

    places = jnp.arange(half, dtype=jnp.int32)
    places = jnp.concatenate([places + core * half, places + (1 - core) * half])
    seg = token_segments(group, places, seq_len, seq_group, seq_start)
    alive = (seg[:half] >= 0).astype(f32)[:, None]

    qkv = (mm(rows_all, qkv_mat) + qkv_bias).astype(bf16)
    context, lse = attn_fwd(qkv, seg)

    def summed_rows(left, right, dims):
        sent = partner(mm(left[half:], right, dims).astype(bf16))
        return mm(left[:half], right, dims) + sent.astype(f32)

    attended = summed_rows(context, out_mat, NT)
    n1, r1 = norm_parts(own.astype(f32) + attended + out_bias)
    first = n1 * gain_one + shift_one
    first_own = first.astype(bf16)
    first_all = jnp.concatenate([first_own, partner(first_own)], axis=0)
    hidden = mm(first_all, up_mat) + up_local
    active = gelu_parts(hidden)[0].astype(bf16)
    branch = summed_rows(active, down_mat, NT)
    n2, r2 = norm_parts(first + branch + down_bias)
    layer_out = turned(((n2 * gain_two + shift_two) * alive).astype(bf16))

    cot = cot_rows.astype(f32) * alive
    d_second = norm_back(cot, n2, r2, gain_two)
    d_branch_own = d_second.astype(bf16)
    d_branch = jnp.concatenate([d_branch_own, partner(d_branch_own)], axis=0)
    d_hidden = (mm(d_branch, down_mat) * gelu_parts(hidden)[1]).astype(bf16)
    part_down = mm(d_branch, active, TN).astype(bf16)
    d_hidden, part_down = lax.optimization_barrier((d_hidden, part_down))
    grad_down = scatter(part_down)
    d_first = d_second + summed_rows(d_hidden, up_mat, NT)
    part_up = mm(first_all, d_hidden, TN).astype(bf16)
    d_first, part_up = lax.optimization_barrier((d_first, part_up))
    grad_up = scatter(part_up)
    d_first_in = norm_back(d_first, n1, r1, gain_one)
    d_attn_own = d_first_in.astype(bf16)
    d_attn = jnp.concatenate([d_attn_own, partner(d_attn_own)], axis=0)
    d_context = mm(d_attn, out_mat).astype(bf16)
    part_out = mm(d_attn, context, TN).astype(bf16)
    d_context, part_out = lax.optimization_barrier((d_context, part_out))
    grad_out = scatter(part_out)
    d_query, d_keys, d_values = attn_bwd(qkv, seg, lse, d_context)
    d_qkv = jnp.concatenate([d_query, d_keys, d_values], axis=1)
    part_qkv = mm(rows_all, d_qkv, TN).astype(bf16)
    d_rows = d_first_in + summed_rows(d_qkv, qkv_mat, NT)
    grad_tokens = turned(d_rows.astype(bf16)).astype(f32)

    def widen(vector):
        total = jnp.zeros((2 * vector.shape[0],), f32)
        return lax.dynamic_update_slice_in_dim(total, vector, core * vector.shape[0], 0)

    sums = (
        widen(jnp.sum(d_query.astype(f32), axis=0)),
        widen(jnp.sum(d_values.astype(f32), axis=0)),
        jnp.sum(d_first_in, axis=0),
        jnp.sum(d_second, axis=0),
        jnp.sum(d_first * n1, axis=0),
        jnp.sum(d_first, axis=0),
        jnp.sum(cot * n2, axis=0),
        jnp.sum(cot, axis=0),
        widen(jnp.sum(d_hidden.astype(f32), axis=0)),
    )
    packed = jnp.concatenate([item.reshape(vectors.shape[0], -1) for item in sums], axis=1)
    packed = (packed + partner(packed)).astype(bf16)
    packed = jnp.pad(packed[:, None, :], ((0, 0), (0, sheet - 1), (0, 3 * width - small_size)))
    part_qkv = part_qkv.reshape(packed.shape[0], shard_rows, 3 * width)
    part_qkv = jnp.concatenate([part_qkv, packed], axis=1)
    grad_qkv = scatter(whole_matrix(part_qkv))
    mine = grad_qkv[shard_rows, :small_size]
    grad_qkv = grad_qkv[:shard_rows]
    parts = [mine[i * piece : (i + 1) * piece] for i in range(8)]
    grad_b_query, grad_b_value, grad_b_out, grad_b_down = parts[:4]
    return (
        layer_out,
        grad_tokens,
        grad_qkv[:, :width],
        grad_qkv[:, width : 2 * width],
        grad_qkv[:, 2 * width :],
        grad_out,
        grad_up,
        grad_down,
        grad_b_query,
        grad_b_value,
        mine[8 * piece :],
        grad_b_out,
        grad_b_down,
        parts[4],
        parts[5],
        parts[6],
        parts[7],
    )


def solution(mesh):
    dp, mp = mesh.devices.shape
    folded = Mesh(mesh.devices.reshape(dp // 2, 2, mp), ("pair", "core", "y"))
    rows = P(("pair", "core", "y"), None)
    weight = P(("pair", "core"), "y")
    vector = P(("pair", "core"))
    placed = (rows,) + (weight,) * 6 + (vector,) * 9 + (rows,) + (P(),) * 3
    return jax.shard_map(
        local,
        mesh=folded,
        in_specs=placed,
        out_specs=(rows, rows) + (weight,) * 6 + (vector,) * 9,
        check_vma=False,
    )
```

```python
import jax
import jax.numpy as jnp
from jax import lax
from jax.experimental import pallas as pl
from jax.experimental.pallas import tpu as pltpu
from jax.sharding import Mesh, PartitionSpec as P

HDIM = 64
PAIR = 2 * HDIM
eps = 1e-05
masked_score = -1e30
scale = HDIM ** (-0.5)
f32 = jnp.float32
bf16 = jnp.bfloat16
NT = (((1,), (1,)), ((), ()))
NN = (((1,), (0,)), ((), ()))
TN = (((0,), (0,)), ((), ()))


def mm(left, right, dims=NN):
    return lax.dot_general(left, right, dims, preferred_element_type=f32)


def head_lanes(rows, head):
    lane = lax.broadcasted_iota(jnp.int32, (rows, PAIR), 1)
    return (lane >= head * HDIM) & (lane < (head + 1) * HDIM)


def attn_fwd_kernel(seg_col, seg_row, q_ref, k_ref, v_ref, ctx_ref, lse_ref):
    rows = q_ref.shape[0]
    same = seg_col[...] == seg_row[...]
    q = q_ref[...] * jnp.asarray(scale, bf16)
    k = k_ref[...]
    v = v_ref[...]
    first = head_lanes(rows, 0)
    parts = []
    for head in range(2):
        qh = jnp.where(head_lanes(rows, head), q, jnp.zeros_like(q))
        scores = jnp.where(same, mm(qh, k, NT), masked_score)
        top = jnp.max(scores, axis=-1, keepdims=True)
        shifted = jnp.exp(scores - top)
        total = jnp.sum(shifted, axis=-1, keepdims=True)
        piece = mm(shifted.astype(bf16), v) * (1.0 / total)
        parts.append((piece, top + jnp.log(total)))
    ctx_ref[...] = jnp.where(first, parts[0][0], parts[1][0]).astype(bf16)
    lse_ref[...] = jnp.where(first, parts[0][1], parts[1][1])


def attn_bwd_kernel(
    seg_col, seg_row, lse_ref, q_ref, k_ref, v_ref, do_ref, dq_ref, dk_ref, dv_ref, dk_acc, dv_acc
):
    block = pl.program_id(1)

    @pl.when(block == 0)
    def _():
        dk_acc[...] = jnp.zeros_like(dk_acc)
        dv_acc[...] = jnp.zeros_like(dv_acc)

    rows = q_ref.shape[0]
    same = seg_col[...] == seg_row[...]
    q = q_ref[...] * jnp.asarray(scale, bf16)
    k = k_ref[...]
    v = v_ref[...]
    do = do_ref[...]
    parts = []
    for head in range(2):
        lanes = head_lanes(rows, head)
        qh = jnp.where(lanes, q, jnp.zeros_like(q))
        doh = jnp.where(lanes, do, jnp.zeros_like(do))
        lse = lse_ref[:, head * HDIM : head * HDIM + 1]
        scores = jnp.where(same, mm(qh, k, NT), masked_score)
        probs = jnp.exp(scores - lse)
        d_probs = mm(doh, v, NT)
        delta = jnp.sum(probs * d_probs, axis=-1, keepdims=True)
        d_scores = (probs * (d_probs - delta)).astype(bf16)
        parts.append(mm(d_scores, k) * scale)
        dk_acc[...] += mm(qh, d_scores, TN)
        dv_acc[...] += mm(doh, probs.astype(bf16), TN)
    dq_ref[...] = jnp.where(head_lanes(rows, 0), parts[0], parts[1]).astype(bf16)

    @pl.when(block == pl.num_programs(1) - 1)
    def _():
        dk_ref[...] = dk_acc[...].T.astype(bf16)
        dv_ref[...] = dv_acc[...].T.astype(bf16)


def attn_specs(rows, pairs, block):
    return (
        pl.BlockSpec((block, 1), lambda h, j: (j, 0)),
        pl.BlockSpec((1, rows), lambda h, j: (0, 0)),
        pl.BlockSpec((block, PAIR), lambda h, j: (j, h)),
        pl.BlockSpec((rows, PAIR), lambda h, j: (0, pairs + h)),
        pl.BlockSpec((rows, PAIR), lambda h, j: (0, 2 * pairs + h)),
    )


def attn_params():
    return pltpu.CompilerParams(
        dimension_semantics=("arbitrary", "arbitrary"), vmem_limit_bytes=56 * 1024 * 1024
    )


def attn_fwd(qkv, seg):
    rows = qkv.shape[0]
    width = qkv.shape[1] // 3
    pairs = width // PAIR
    block = min(512, rows)
    col, row, qs, ks, vs = attn_specs(rows, pairs, block)
    per_block = pl.BlockSpec((block, PAIR), lambda h, j: (j, h))
    return pl.pallas_call(
        attn_fwd_kernel,
        grid=(pairs, rows // block),
        in_specs=[col, row, qs, ks, vs],
        out_specs=[per_block, per_block],
        out_shape=[
            jax.ShapeDtypeStruct((rows, width), bf16),
            jax.ShapeDtypeStruct((rows, width), f32),
        ],
        compiler_params=attn_params(),
        cost_estimate=pl.CostEstimate(
            flops=8 * rows * rows * width,
            bytes_accessed=rows * width * 12,
            transcendentals=rows * rows * width // HDIM,
        ),
        name="attn_fwd",
    )(seg[:, None], seg[None, :], qkv, qkv, qkv)


def attn_bwd(qkv, seg, lse, do):
    rows = qkv.shape[0]
    width = qkv.shape[1] // 3
    pairs = width // PAIR
    block = min(512, rows)
    col, row, qs, ks, vs = attn_specs(rows, pairs, block)
    per_block = pl.BlockSpec((block, PAIR), lambda h, j: (j, h))
    whole = pl.BlockSpec((rows, PAIR), lambda h, j: (0, h))
    return pl.pallas_call(
        attn_bwd_kernel,
        grid=(pairs, rows // block),
        in_specs=[col, row, per_block, qs, ks, vs, per_block],
        out_specs=[per_block, whole, whole],
        out_shape=[jax.ShapeDtypeStruct((rows, width), bf16)] * 3,
        scratch_shapes=[pltpu.VMEM((PAIR, rows), f32), pltpu.VMEM((PAIR, rows), f32)],
        compiler_params=attn_params(),
        cost_estimate=pl.CostEstimate(
            flops=20 * rows * rows * width,
            bytes_accessed=rows * width * 18,
            transcendentals=rows * rows * width // HDIM,
        ),
        name="attn_bwd",
    )(seg[:, None], seg[None, :], lse, qkv, qkv, qkv, do)


def norm_parts(values):
    center = values - jnp.mean(values, axis=-1, keepdims=True)
    factor = lax.rsqrt(jnp.mean(center * center, axis=-1, keepdims=True) + eps)
    return center * factor, factor


def norm_back(cot, normed, factor, gain):
    e = cot * gain
    mean_e = jnp.mean(e, axis=-1, keepdims=True)
    mean_en = jnp.mean(e * normed, axis=-1, keepdims=True)
    return factor * (e - mean_e - normed * mean_en)


def token_segments(group_id, places, seq_len, seq_group, seq_start):
    places = places[None, :]
    starts = seq_start[:, None]
    inside = (
        (seq_group[:, None] == group_id) & (places >= starts) & (places < starts + seq_len[:, None])
    )
    labels = jnp.arange(1, seq_len.shape[0] + 1, dtype=jnp.int32)[:, None]
    return jnp.sum(jnp.where(inside, labels, 0), axis=0) - 1


def gelu_parts(hidden):
    cdf = 0.5 * (1.0 + lax.erf(hidden * (0.5**0.5)))
    slope = cdf + hidden * jnp.exp(-0.5 * hidden * hidden) * (0.5 / jnp.pi) ** 0.5
    return hidden * cdf, slope


def turned(x):
    return lax.ppermute(x, ("core", "y"), [(0, 0), (1, 2), (2, 1), (3, 3)])


def partner(x):
    return lax.ppermute(x, "core", [(0, 1), (1, 0)])


def local(
    tokens,
    w_query,
    w_key,
    w_value,
    w_out,
    w_up,
    w_down,
    b_query,
    b_value,
    b_up,
    b_out,
    b_down,
    gain_attn,
    shift_attn,
    gain_ffn,
    shift_ffn,
    out_grad,
    seq_len,
    seq_group,
    seq_start,
):
    half = tokens.shape[0]
    core = lax.axis_index("core")
    group = lax.axis_index("pair") * 2 + lax.axis_index("y")
    width = w_query.shape[1]
    hidden_width = w_up.shape[1]

    side = lax.axis_index("y")
    pairs = lax.axis_size("pair")
    sheet = 16

    def across(x):
        return lax.ppermute(x, "y", [(0, 1), (1, 0)])

    def gather(x):
        shard = turned(x)
        mine = lax.all_gather(shard, "pair", axis=0, tiled=False)
        other = across(mine)
        low = jnp.where(side == 0, mine, other)
        high = jnp.where(side == 0, other, mine)
        return jnp.stack([low, high], axis=1)

    def scatter(x):
        blocks = x.reshape(pairs, 2, -1, x.shape[-1])
        sent = across(lax.dynamic_index_in_dim(blocks, 1 - side, 1, keepdims=False))
        kept = lax.dynamic_index_in_dim(blocks, side, 1, keepdims=False)
        total = (kept.astype(f32) + sent.astype(f32)).astype(bf16)
        total = total.reshape(-1, x.shape[-1])
        part = lax.psum_scatter(total, "pair", scatter_dimension=0, tiled=True)
        return turned(part).astype(f32)

    def whole_matrix(x):
        return x.reshape(-1, x.shape[-1])

    shard_rows = w_query.shape[0]
    small = (b_query, b_value, b_out, b_down, gain_attn, shift_attn, gain_ffn, shift_ffn, b_up)
    small = jnp.concatenate(small)
    small_size = small.shape[0]
    extra = jnp.pad(small[None, :], ((0, sheet - 1), (0, 4 * width - small_size)))
    qkv_shard = jnp.concatenate([w_query, w_key, w_value, w_out], axis=1)
    qkv_full = gather(jnp.concatenate([qkv_shard, extra], axis=0))
    qkv_mat = whole_matrix(qkv_full[:, :, :shard_rows, : 3 * width])
    out_mat = whole_matrix(qkv_full[:, :, :shard_rows, 3 * width :])
    vectors = qkv_full[:, :, shard_rows, :small_size].reshape(-1, small_size)
    own = turned(tokens)
    rows_all = jnp.concatenate([own, partner(own)], axis=0)
    up_mat = whole_matrix(gather(w_up))
    down_mat = whole_matrix(gather(w_down))
    cot_rows = turned(out_grad)

    piece = b_query.shape[0]
    full = [
        vectors[:, i * piece : (i + 1) * piece].reshape(-1).astype(f32) for i in range(8)
    ]
    up_bias = vectors[:, 8 * piece :].reshape(-1).astype(f32)
    query_bias, value_bias, out_bias, down_bias, gain_one, shift_one, gain_two, shift_two = full
    query_local = lax.dynamic_slice_in_dim(query_bias, core * width, width)
    value_local = lax.dynamic_slice_in_dim(value_bias, core * width, width)
    up_local = lax.dynamic_slice_in_dim(up_bias, core * hidden_width, hidden_width)
    qkv_bias = jnp.concatenate([query_local, jnp.zeros((width,), f32), value_local])

    places = jnp.arange(half, dtype=jnp.int32)
    places = jnp.concatenate([places + core * half, places + (1 - core) * half])
    seg = token_segments(group, places, seq_len, seq_group, seq_start)
    alive = (seg[:half] >= 0).astype(f32)[:, None]

    qkv = (mm(rows_all, qkv_mat) + qkv_bias).astype(bf16)
    context, lse = attn_fwd(qkv, seg)

    def summed_rows(left, right, dims):
        sent = partner(mm(left[half:], right, dims).astype(bf16))
        return mm(left[:half], right, dims) + sent.astype(f32)

    attended = summed_rows(context, out_mat, NT)
    n1, r1 = norm_parts(own.astype(f32) + attended + out_bias)
    first = n1 * gain_one + shift_one
    first_own = first.astype(bf16)
    first_all = jnp.concatenate([first_own, partner(first_own)], axis=0)
    hidden = mm(first_all, up_mat) + up_local
    active = gelu_parts(hidden)[0].astype(bf16)
    branch = summed_rows(active, down_mat, NT)
    n2, r2 = norm_parts(first + branch + down_bias)
    layer_out = turned(((n2 * gain_two + shift_two) * alive).astype(bf16))

    cot = cot_rows.astype(f32) * alive
    d_second = norm_back(cot, n2, r2, gain_two)
    d_branch_own = d_second.astype(bf16)
    d_branch = jnp.concatenate([d_branch_own, partner(d_branch_own)], axis=0)
    d_hidden = (mm(d_branch, down_mat) * gelu_parts(hidden)[1]).astype(bf16)
    part_down = mm(d_branch, active, TN).astype(bf16)
    d_hidden, part_down = lax.optimization_barrier((d_hidden, part_down))
    grad_down = scatter(part_down)
    d_first = d_second + summed_rows(d_hidden, up_mat, NT)
    part_up = mm(first_all, d_hidden, TN).astype(bf16)
    d_first, part_up = lax.optimization_barrier((d_first, part_up))
    grad_up = scatter(part_up)
    d_first_in = norm_back(d_first, n1, r1, gain_one)
    d_attn_own = d_first_in.astype(bf16)
    d_attn = jnp.concatenate([d_attn_own, partner(d_attn_own)], axis=0)
    d_context = mm(d_attn, out_mat).astype(bf16)
    part_out = mm(d_attn, context, TN).astype(bf16)
    d_context, part_out = lax.optimization_barrier((d_context, part_out))
    d_query, d_keys, d_values = attn_bwd(qkv, seg, lse, d_context)
    d_qkv = jnp.concatenate([d_query, d_keys, d_values], axis=1)
    part_qkv = mm(rows_all, d_qkv, TN).astype(bf16)
    part_qkv = jnp.concatenate([part_qkv, part_out], axis=1)
    d_rows = d_first_in + summed_rows(d_qkv, qkv_mat, NT)
    grad_tokens = turned(d_rows.astype(bf16)).astype(f32)

    def widen(vector):
        total = jnp.zeros((2 * vector.shape[0],), f32)
        return lax.dynamic_update_slice_in_dim(total, vector, core * vector.shape[0], 0)

    sums = (
        widen(jnp.sum(d_query.astype(f32), axis=0)),
        widen(jnp.sum(d_values.astype(f32), axis=0)),
        jnp.sum(d_first_in, axis=0),
        jnp.sum(d_second, axis=0),
        jnp.sum(d_first * n1, axis=0),
        jnp.sum(d_first, axis=0),
        jnp.sum(cot * n2, axis=0),
        jnp.sum(cot, axis=0),
        widen(jnp.sum(d_hidden.astype(f32), axis=0)),
    )
    packed = jnp.concatenate([item.reshape(vectors.shape[0], -1) for item in sums], axis=1)
    packed = (packed + partner(packed)).astype(bf16)
    packed = jnp.pad(packed[:, None, :], ((0, 0), (0, sheet - 1), (0, 4 * width - small_size)))
    part_qkv = part_qkv.reshape(packed.shape[0], shard_rows, 4 * width)
    part_qkv = jnp.concatenate([part_qkv, packed], axis=1)
    grad_qkv = scatter(whole_matrix(part_qkv))
    mine = grad_qkv[shard_rows, :small_size]
    grad_qkv = grad_qkv[:shard_rows]
    parts = [mine[i * piece : (i + 1) * piece] for i in range(8)]
    grad_b_query, grad_b_value, grad_b_out, grad_b_down = parts[:4]
    return (
        layer_out,
        grad_tokens,
        grad_qkv[:, :width],
        grad_qkv[:, width : 2 * width],
        grad_qkv[:, 2 * width : 3 * width],
        grad_qkv[:, 3 * width :],
        grad_up,
        grad_down,
        grad_b_query,
        grad_b_value,
        mine[8 * piece :],
        grad_b_out,
        grad_b_down,
        parts[4],
        parts[5],
        parts[6],
        parts[7],
    )


def solution(mesh):
    dp, mp = mesh.devices.shape
    folded = Mesh(mesh.devices.reshape(dp // 2, 2, mp), ("pair", "core", "y"))
    rows = P(("pair", "core", "y"), None)
    weight = P(("pair", "core"), "y")
    vector = P(("pair", "core"))
    placed = (rows,) + (weight,) * 6 + (vector,) * 9 + (rows,) + (P(),) * 3
    return jax.shard_map(
        local,
        mesh=folded,
        in_specs=placed,
        out_specs=(rows, rows) + (weight,) * 6 + (vector,) * 9,
        check_vma=False,
    )
```

```python
import jax
import jax.numpy as jnp
from jax import lax
from jax.experimental import pallas as pl
from jax.experimental.pallas import tpu as pltpu
from jax.sharding import Mesh, PartitionSpec as P

HDIM = 64
PAIR = 2 * HDIM
eps = 1e-05
masked_score = -1e30
scale = HDIM ** (-0.5)
f32 = jnp.float32
bf16 = jnp.bfloat16
NT = (((1,), (1,)), ((), ()))
NN = (((1,), (0,)), ((), ()))
TN = (((0,), (0,)), ((), ()))


def mm(left, right, dims=NN):
    return lax.dot_general(left, right, dims, preferred_element_type=f32)


def head_lanes(rows, head):
    lane = lax.broadcasted_iota(jnp.int32, (rows, PAIR), 1)
    return (lane >= head * HDIM) & (lane < (head + 1) * HDIM)


def attn_fwd_kernel(seg_col, seg_row, q_ref, k_ref, v_ref, ctx_ref, lse_ref):
    rows = q_ref.shape[0]
    same = seg_col[...] == seg_row[...]
    q = q_ref[...] * jnp.asarray(scale, bf16)
    k = k_ref[...]
    v = v_ref[...]
    first = head_lanes(rows, 0)
    parts = []
    for head in range(2):
        qh = jnp.where(head_lanes(rows, head), q, jnp.zeros_like(q))
        scores = jnp.where(same, mm(qh, k, NT), masked_score)
        top = jnp.max(scores, axis=-1, keepdims=True)
        shifted = jnp.exp(scores - top)
        total = jnp.sum(shifted, axis=-1, keepdims=True)
        piece = mm(shifted.astype(bf16), v) * (1.0 / total)
        parts.append((piece, top + jnp.log(total)))
    ctx_ref[...] = jnp.where(first, parts[0][0], parts[1][0]).astype(bf16)
    lse_ref[...] = jnp.where(first, parts[0][1], parts[1][1])


def attn_bwd_kernel(
    seg_col, seg_row, lse_ref, q_ref, k_ref, v_ref, do_ref, dq_ref, dk_ref, dv_ref, dk_acc, dv_acc
):
    block = pl.program_id(1)

    @pl.when(block == 0)
    def _():
        dk_acc[...] = jnp.zeros_like(dk_acc)
        dv_acc[...] = jnp.zeros_like(dv_acc)

    rows = q_ref.shape[0]
    same = seg_col[...] == seg_row[...]
    q = q_ref[...] * jnp.asarray(scale, bf16)
    k = k_ref[...]
    v = v_ref[...]
    do = do_ref[...]
    parts = []
    for head in range(2):
        lanes = head_lanes(rows, head)
        qh = jnp.where(lanes, q, jnp.zeros_like(q))
        doh = jnp.where(lanes, do, jnp.zeros_like(do))
        lse = lse_ref[:, head * HDIM : head * HDIM + 1]
        scores = jnp.where(same, mm(qh, k, NT), masked_score)
        probs = jnp.exp(scores - lse)
        d_probs = mm(doh, v, NT)
        delta = jnp.sum(probs * d_probs, axis=-1, keepdims=True)
        d_scores = (probs * (d_probs - delta)).astype(bf16)
        parts.append(mm(d_scores, k) * scale)
        dk_acc[...] += mm(qh, d_scores, TN)
        dv_acc[...] += mm(doh, probs.astype(bf16), TN)
    dq_ref[...] = jnp.where(head_lanes(rows, 0), parts[0], parts[1]).astype(bf16)

    @pl.when(block == pl.num_programs(1) - 1)
    def _():
        dk_ref[...] = dk_acc[...].T.astype(bf16)
        dv_ref[...] = dv_acc[...].T.astype(bf16)


def attn_specs(rows, pairs, block):
    return (
        pl.BlockSpec((block, 1), lambda h, j: (j, 0)),
        pl.BlockSpec((1, rows), lambda h, j: (0, 0)),
        pl.BlockSpec((block, PAIR), lambda h, j: (j, h)),
        pl.BlockSpec((rows, PAIR), lambda h, j: (0, pairs + h)),
        pl.BlockSpec((rows, PAIR), lambda h, j: (0, 2 * pairs + h)),
    )


def attn_params():
    return pltpu.CompilerParams(
        dimension_semantics=("arbitrary", "arbitrary"), vmem_limit_bytes=56 * 1024 * 1024
    )


def attn_fwd(qkv, seg):
    rows = qkv.shape[0]
    width = qkv.shape[1] // 3
    pairs = width // PAIR
    block = min(512, rows)
    col, row, qs, ks, vs = attn_specs(rows, pairs, block)
    per_block = pl.BlockSpec((block, PAIR), lambda h, j: (j, h))
    return pl.pallas_call(
        attn_fwd_kernel,
        grid=(pairs, rows // block),
        in_specs=[col, row, qs, ks, vs],
        out_specs=[per_block, per_block],
        out_shape=[
            jax.ShapeDtypeStruct((rows, width), bf16),
            jax.ShapeDtypeStruct((rows, width), f32),
        ],
        compiler_params=attn_params(),
        cost_estimate=pl.CostEstimate(
            flops=8 * rows * rows * width,
            bytes_accessed=rows * width * 12,
            transcendentals=rows * rows * width // HDIM,
        ),
        name="attn_fwd",
    )(seg[:, None], seg[None, :], qkv, qkv, qkv)


def attn_bwd(qkv, seg, lse, do):
    rows = qkv.shape[0]
    width = qkv.shape[1] // 3
    pairs = width // PAIR
    block = min(512, rows)
    col, row, qs, ks, vs = attn_specs(rows, pairs, block)
    per_block = pl.BlockSpec((block, PAIR), lambda h, j: (j, h))
    whole = pl.BlockSpec((rows, PAIR), lambda h, j: (0, h))
    return pl.pallas_call(
        attn_bwd_kernel,
        grid=(pairs, rows // block),
        in_specs=[col, row, per_block, qs, ks, vs, per_block],
        out_specs=[per_block, whole, whole],
        out_shape=[jax.ShapeDtypeStruct((rows, width), bf16)] * 3,
        scratch_shapes=[pltpu.VMEM((PAIR, rows), f32), pltpu.VMEM((PAIR, rows), f32)],
        compiler_params=attn_params(),
        cost_estimate=pl.CostEstimate(
            flops=20 * rows * rows * width,
            bytes_accessed=rows * width * 18,
            transcendentals=rows * rows * width // HDIM,
        ),
        name="attn_bwd",
    )(seg[:, None], seg[None, :], lse, qkv, qkv, qkv, do)


def norm_parts(values):
    center = values - jnp.mean(values, axis=-1, keepdims=True)
    factor = lax.rsqrt(jnp.mean(center * center, axis=-1, keepdims=True) + eps)
    return center * factor, factor


def norm_back(cot, normed, factor, gain):
    e = cot * gain
    mean_e = jnp.mean(e, axis=-1, keepdims=True)
    mean_en = jnp.mean(e * normed, axis=-1, keepdims=True)
    return factor * (e - mean_e - normed * mean_en)


def token_segments(group_id, places, seq_len, seq_group, seq_start):
    places = places[None, :]
    starts = seq_start[:, None]
    inside = (
        (seq_group[:, None] == group_id) & (places >= starts) & (places < starts + seq_len[:, None])
    )
    labels = jnp.arange(1, seq_len.shape[0] + 1, dtype=jnp.int32)[:, None]
    return jnp.sum(jnp.where(inside, labels, 0), axis=0) - 1


def gelu_parts(hidden):
    cdf = 0.5 * (1.0 + lax.erf(hidden * (0.5**0.5)))
    slope = cdf + hidden * jnp.exp(-0.5 * hidden * hidden) * (0.5 / jnp.pi) ** 0.5
    return hidden * cdf, slope


def turned(x):
    return lax.ppermute(x, ("core", "y"), [(0, 0), (1, 2), (2, 1), (3, 3)])


def partner(x):
    return lax.ppermute(x, "core", [(0, 1), (1, 0)])


def local(
    tokens,
    w_query,
    w_key,
    w_value,
    w_out,
    w_up,
    w_down,
    b_query,
    b_value,
    b_up,
    b_out,
    b_down,
    gain_attn,
    shift_attn,
    gain_ffn,
    shift_ffn,
    out_grad,
    seq_len,
    seq_group,
    seq_start,
):
    half = tokens.shape[0]
    core = lax.axis_index("core")
    group = lax.axis_index("pair") * 2 + lax.axis_index("y")
    width = w_query.shape[1]
    hidden_width = w_up.shape[1]

    side = lax.axis_index("y")
    pairs = lax.axis_size("pair")
    sheet = 16

    def across(x):
        return lax.ppermute(x, "y", [(0, 1), (1, 0)])

    def gather(x):
        shard = turned(x)
        mine = lax.all_gather(shard, "pair", axis=0, tiled=False)
        other = across(mine)
        low = jnp.where(side == 0, mine, other)
        high = jnp.where(side == 0, other, mine)
        return jnp.stack([low, high], axis=1)

    def halve(x):
        blocks = x.reshape(pairs, 2, -1, x.shape[-1])
        sent = across(lax.dynamic_index_in_dim(blocks, 1 - side, 1, keepdims=False))
        kept = lax.dynamic_index_in_dim(blocks, side, 1, keepdims=False)
        total = (kept.astype(f32) + sent.astype(f32)).astype(bf16)
        return total.reshape(-1, x.shape[-1])

    def finish(total):
        part = lax.psum_scatter(total, "pair", scatter_dimension=0, tiled=True)
        return turned(part).astype(f32)

    def whole_matrix(x):
        return x.reshape(-1, x.shape[-1])

    shard_rows = w_query.shape[0]
    small = (b_query, b_value, b_out, b_down, gain_attn, shift_attn, gain_ffn, shift_ffn, b_up)
    small = jnp.concatenate(small)
    small_size = small.shape[0]
    extra = jnp.pad(small[None, :], ((0, sheet - 1), (0, 4 * width - small_size)))
    qkv_shard = jnp.concatenate([w_query, w_key, w_value, w_out], axis=1)
    qkv_full = gather(jnp.concatenate([qkv_shard, extra], axis=0))
    qkv_mat = whole_matrix(qkv_full[:, :, :shard_rows, : 3 * width])
    out_mat = whole_matrix(qkv_full[:, :, :shard_rows, 3 * width :])
    vectors = qkv_full[:, :, shard_rows, :small_size].reshape(-1, small_size)
    own = turned(tokens)
    rows_all = jnp.concatenate([own, partner(own)], axis=0)
    up_mat = whole_matrix(gather(w_up))
    down_mat = whole_matrix(gather(w_down))
    cot_rows = turned(out_grad)

    piece = b_query.shape[0]
    full = [
        vectors[:, i * piece : (i + 1) * piece].reshape(-1).astype(f32) for i in range(8)
    ]
    up_bias = vectors[:, 8 * piece :].reshape(-1).astype(f32)
    query_bias, value_bias, out_bias, down_bias, gain_one, shift_one, gain_two, shift_two = full
    query_local = lax.dynamic_slice_in_dim(query_bias, core * width, width)
    value_local = lax.dynamic_slice_in_dim(value_bias, core * width, width)
    up_local = lax.dynamic_slice_in_dim(up_bias, core * hidden_width, hidden_width)
    qkv_bias = jnp.concatenate([query_local, jnp.zeros((width,), f32), value_local])

    places = jnp.arange(half, dtype=jnp.int32)
    places = jnp.concatenate([places + core * half, places + (1 - core) * half])
    seg = token_segments(group, places, seq_len, seq_group, seq_start)
    alive = (seg[:half] >= 0).astype(f32)[:, None]

    qkv = (mm(rows_all, qkv_mat) + qkv_bias).astype(bf16)
    context, lse = attn_fwd(qkv, seg)

    def summed_rows(left, right, dims):
        sent = partner(mm(left[half:], right, dims).astype(bf16))
        return mm(left[:half], right, dims) + sent.astype(f32)

    attended = summed_rows(context, out_mat, NT)
    n1, r1 = norm_parts(own.astype(f32) + attended + out_bias)
    first = n1 * gain_one + shift_one
    first_own = first.astype(bf16)
    first_all = jnp.concatenate([first_own, partner(first_own)], axis=0)
    hidden = mm(first_all, up_mat) + up_local
    active = gelu_parts(hidden)[0].astype(bf16)
    branch = summed_rows(active, down_mat, NT)
    n2, r2 = norm_parts(first + branch + down_bias)
    layer_out = turned(((n2 * gain_two + shift_two) * alive).astype(bf16))

    cot = cot_rows.astype(f32) * alive
    d_second = norm_back(cot, n2, r2, gain_two)
    d_branch_own = d_second.astype(bf16)
    d_branch = jnp.concatenate([d_branch_own, partner(d_branch_own)], axis=0)
    d_hidden = (mm(d_branch, down_mat) * gelu_parts(hidden)[1]).astype(bf16)
    part_down = mm(d_branch, active, TN).astype(bf16)
    d_hidden, part_down = lax.optimization_barrier((d_hidden, part_down))
    half_down = halve(part_down)
    d_first = d_second + summed_rows(d_hidden, up_mat, NT)
    part_up = mm(first_all, d_hidden, TN).astype(bf16)
    d_first, part_up = lax.optimization_barrier((d_first, part_up))
    half_up = halve(part_up)
    d_first_in = norm_back(d_first, n1, r1, gain_one)
    d_attn_own = d_first_in.astype(bf16)
    d_attn = jnp.concatenate([d_attn_own, partner(d_attn_own)], axis=0)
    d_context = mm(d_attn, out_mat).astype(bf16)
    part_out = mm(d_attn, context, TN).astype(bf16)
    d_context, part_out, half_down = lax.optimization_barrier((d_context, part_out, half_down))
    grad_down = finish(half_down)
    d_query, d_keys, d_values = attn_bwd(qkv, seg, lse, d_context)
    d_query, half_up = lax.optimization_barrier((d_query, half_up))
    grad_up = finish(half_up)
    d_qkv = jnp.concatenate([d_query, d_keys, d_values], axis=1)
    part_qkv = mm(rows_all, d_qkv, TN).astype(bf16)
    part_qkv = jnp.concatenate([part_qkv, part_out], axis=1)
    d_rows = d_first_in + summed_rows(d_qkv, qkv_mat, NT)
    grad_tokens = turned(d_rows.astype(bf16)).astype(f32)

    def widen(vector):
        total = jnp.zeros((2 * vector.shape[0],), f32)
        return lax.dynamic_update_slice_in_dim(total, vector, core * vector.shape[0], 0)

    sums = (
        widen(jnp.sum(d_query.astype(f32), axis=0)),
        widen(jnp.sum(d_values.astype(f32), axis=0)),
        jnp.sum(d_first_in, axis=0),
        jnp.sum(d_second, axis=0),
        jnp.sum(d_first * n1, axis=0),
        jnp.sum(d_first, axis=0),
        jnp.sum(cot * n2, axis=0),
        jnp.sum(cot, axis=0),
        widen(jnp.sum(d_hidden.astype(f32), axis=0)),
    )
    packed = jnp.concatenate([item.reshape(vectors.shape[0], -1) for item in sums], axis=1)
    packed = (packed + partner(packed)).astype(bf16)
    packed = jnp.pad(packed[:, None, :], ((0, 0), (0, sheet - 1), (0, 4 * width - small_size)))
    part_qkv = part_qkv.reshape(packed.shape[0], shard_rows, 4 * width)
    part_qkv = jnp.concatenate([part_qkv, packed], axis=1)
    grad_qkv = finish(halve(whole_matrix(part_qkv)))
    mine = grad_qkv[shard_rows, :small_size]
    grad_qkv = grad_qkv[:shard_rows]
    parts = [mine[i * piece : (i + 1) * piece] for i in range(8)]
    grad_b_query, grad_b_value, grad_b_out, grad_b_down = parts[:4]
    return (
        layer_out,
        grad_tokens,
        grad_qkv[:, :width],
        grad_qkv[:, width : 2 * width],
        grad_qkv[:, 2 * width : 3 * width],
        grad_qkv[:, 3 * width :],
        grad_up,
        grad_down,
        grad_b_query,
        grad_b_value,
        mine[8 * piece :],
        grad_b_out,
        grad_b_down,
        parts[4],
        parts[5],
        parts[6],
        parts[7],
    )


def solution(mesh):
    dp, mp = mesh.devices.shape
    folded = Mesh(mesh.devices.reshape(dp // 2, 2, mp), ("pair", "core", "y"))
    rows = P(("pair", "core", "y"), None)
    weight = P(("pair", "core"), "y")
    vector = P(("pair", "core"))
    placed = (rows,) + (weight,) * 6 + (vector,) * 9 + (rows,) + (P(),) * 3
    return jax.shard_map(
        local,
        mesh=folded,
        in_specs=placed,
        out_specs=(rows, rows) + (weight,) * 6 + (vector,) * 9,
        check_vma=False,
    )
```
